128 devices in a mesh: group: 2 (over x_hi), expert: 64 (over x_lo, y, z, core).
Axes of the slice: x: 4 (x_hi: 2, x_lo: 2; x = x_hi * 2 + x_lo), y: 4, z: 4, core: 2. Of those that a mesh axis runs over, the one named last changes fastest.
Arguments:
- tokens: bfloat16 [2, 8192, 4096], P('group', 'expert'), may hold values from -6 to 6
- expert_ids: int32 [2, 8192, 1], P('group', 'expert'), may hold values from 0 to 7; in each aligned block of 128 rows (0 to 127, 128 to 255, ..., all dimensions but the last counted through in order) at most 32 rows name the same one
- route_weight: float32 [2, 8192, 1], P('group', 'expert'), may hold values from 0.1 to 1
- inner_weights: bfloat16 [2, 3, 12288, 4096], P('group', None, 'expert'), may hold values from -0.09375 to 0.09375
- outer_weights: float32 [3, 12288, 4096], P(None, 'expert', 'group'), may hold values from -0.09375 to 0.09375
- momentum: float32 [3, 12288, 4096], P(None, 'expert', 'group'), may hold values from -0.09375 to 0.09375
Outputs:
- expert_out: bfloat16 [2, 8192, 4096], P('group', 'expert')
- new_outer: float32 [3, 12288, 4096], P(None, 'expert', 'group')
- new_momentum: float32 [3, 12288, 4096], P(None, 'expert', 'group')
The draws below stay inside these ranges and needn't reach their ends.
Inputs may be any that keep to these rules, and one draw needn't show every extreme that they name: `expert_ids`: among the tokens of one device, no expert is named more than 32 times, and in every draw some device has an expert named exactly 32 times.
All inputs are finite; a program needn't handle non-finite values.
Results may differ from the reference program's by a relative error of at most 0.025.
Values may be sent and summed in bfloat16 or wider, within the bound.
A program may use at most 192 MiB of HBM per device.

```python
import math
import jax
import jax.numpy as jnp
import numpy as np
from jax import lax

D = 4096
F = 1536
SPLIT = 8
PICKS = 1
TOK_DEV = 128
F_DEV = 192
EXPERTS = 8
TOKENS = 8192
CAP = 32
N_GROUP = 2
N_EXPERT = 64


def steps_of(own_key, shape, split, low, largest):
    def one(position, shards_of):
        draws = jax.random.uniform(jax.random.fold_in(jax.random.fold_in(own_key, 6), position), (shards_of,), jnp.float32, low / len(split), largest / len(split))
        return jnp.repeat(jnp.exp(draws), shape[position] // shards_of).reshape((-1,) + (1,) * (len(shape) - position - 1))

    gain = one(*split[0])
    for cut in split[1:]:
        gain = gain * one(*cut)
    return gain


def routed_block(key, own, number, rows, amount, top, bound, lean):
    sequence = jax.random.permutation(key, amount)
    crowded, common = shares(amount, rows * top, bound, lean, True), shares(amount, rows * top, bound, lean, False)
    places = jnp.arange(amount)

    def named(sizes, offset_by):
        used = int((sizes > 0).sum())
        fixed = max(1, used // 4)
        shifted = fixed + (places - fixed + offset_by * (used - fixed)) % max(1, amount - fixed)
        return jnp.zeros((amount,), jnp.int32).at[sequence[jnp.where(places < fixed, places, shifted)]].set(jnp.asarray(sizes, jnp.int32))

    sizes = jnp.where(number % 4 == 0, named(crowded, number // 4), named(common, number - number // 4 - 1))
    mixed = jax.random.permutation(jax.random.fold_in(own, 3), amount)
    donor, taker = mixed[0:amount // 2 * 2:2], mixed[1:amount // 2 * 2:2]
    slack = jnp.minimum(sizes[donor] - 1, bound - sizes[taker]) // 2
    slack = jnp.where((donor == sequence[0]) | (taker == sequence[0]) | (sizes[taker] == 0), 0, jnp.maximum(slack, 0))
    shifted = jax.random.randint(jax.random.fold_in(own, 4), (amount // 2,), 0, 1 << 20) % (slack + 1)
    sizes = sizes.at[donor].add(-shifted).at[taker].add(shifted)
    labels = jnp.searchsorted(jnp.cumsum(sizes), jnp.arange(rows * top), side="right").astype(jnp.int32)
    table = labels.reshape(top, rows).T
    table = table[jax.random.permutation(jax.random.fold_in(own, 1), rows)]
    offset_by = jax.random.randint(jax.random.fold_in(own, 2), (rows, 1), 0, top)
    return jnp.take_along_axis(table, (jnp.arange(top)[None, :] + offset_by) % top, axis=1)


def shares(amount, total, most, slope, full):
    weights = [(1 << 20) // math.isqrt(standing ** slope) + 1 for standing in range(1, amount + 1)]
    largest = most if full else min(most, max(-(-total // amount), total * weights[0] // sum(weights)))
    least = 1 if total - largest >= amount - 1 else 0
    holding, rest = [largest] + [least] * (amount - 1), total - largest - least * (amount - 1)
    while rest > 0:
        free = [i for i in range(1, amount) if holding[i] < largest] or [i for i in range(1, amount) if holding[i] < most]
        whole, remaining = sum([weights[i] for i in free]), rest
        for i in free:
            more = min(most - holding[i], max(1, remaining * weights[i] // whole), rest)
            holding[i] = holding[i] + more
            rest = rest - more
    return np.array(holding)


def bell_draw(stream_key, shape, deviation, most, cuts=(), kind=jnp.bfloat16):
    array = deviation * jax.random.normal(stream_key, shape, jnp.float32)
    if cuts:
        array = array * steps_of(stream_key, shape, cuts, -0.22, 0.18)
    return jnp.clip(array, -most, most).astype(kind)


def setup_inputs(seed: int = 0) -> dict:
    key_of = jax.random.split(jax.random.key(seed), 7)
    tokens = bell_draw(key_of[0], (N_GROUP, TOKENS, D), 1.0, 6.0, ((0, 2), (1, 64)))
    expert_ids_keys = jax.random.split(jax.random.fold_in(key_of[1], 1), N_GROUP * TOKENS // TOK_DEV)
    expert_ids_turns = jax.random.permutation(jax.random.fold_in(key_of[1], 3), N_GROUP * TOKENS // TOK_DEV)
    expert_ids = jax.vmap(lambda own, number: routed_block(jax.random.fold_in(key_of[1], 2), own, number, TOK_DEV, EXPERTS, PICKS, CAP, 2))(expert_ids_keys, expert_ids_turns).reshape((N_GROUP, TOKENS, PICKS))
    route_weight = jnp.clip(0.1 + 0.9 * jax.random.uniform(key_of[2], (N_GROUP, TOKENS, PICKS), jnp.float32) ** steps_of(key_of[2], (N_GROUP, TOKENS, PICKS), ((0, 2), (1, 64)), -0.2, 0.2), 0.1, 1.0)
    inner_weights = bell_draw(key_of[3], (N_GROUP, 3, EXPERTS * F, D), D ** -0.5, 0.09375, ((0, 2), (2, 64)))
    outer_weights = bell_draw(key_of[4], (3, EXPERTS * F, D), D ** -0.5, 0.09375, ((1, 64), (2, 2)), jnp.float32)
    momentum = bell_draw(key_of[5], (3, EXPERTS * F, D), D ** -0.5, 0.09375, ((1, 64), (2, 2)), jnp.float32)
    return dict(tokens=tokens, expert_ids=expert_ids, route_weight=route_weight, inner_weights=inner_weights, outer_weights=outer_weights, momentum=momentum)


outer_rate = 0.7
momentum_rate = 0.9


def expert_block(operands):
    rows_in, weights = operands
    dims = (((1,), (1,)), ((), ()))
    gate = lax.dot_general(rows_in, weights[0], dims, preferred_element_type=jnp.float32)
    upward = lax.dot_general(rows_in, weights[1], dims, preferred_element_type=jnp.float32)
    hidden = (jax.nn.silu(gate) * upward).astype(jnp.bfloat16)
    sliced = hidden.reshape(rows_in.shape[0], SPLIT, F_DEV).astype(jnp.float32)
    down_sliced = weights[2].reshape(SPLIT, F_DEV, D).astype(jnp.float32)
    partial_value = jnp.einsum("rsf,sfd->srd", sliced, down_sliced).astype(jnp.bfloat16)
    partial_value = lax.optimization_barrier(partial_value)
    return jnp.sum(partial_value.astype(jnp.float32), axis=0)


def reference(tokens, expert_ids, route_weight, inner_weights, outer_weights, momentum):
    mean_inner = jnp.sum(inner_weights.astype(jnp.float32), axis=0) / N_GROUP
    pseudo = outer_weights - mean_inner
    new_momentum = momentum_rate * momentum + pseudo
    new_outer = outer_weights - outer_rate * (pseudo + momentum_rate * new_momentum)
    fresh = new_outer.astype(jnp.bfloat16).reshape(3, EXPERTS, F, D)
    per_expert = jnp.transpose(fresh, (1, 0, 2, 3))
    buffer_rows = N_EXPERT * CAP
    outputs = []
    for group_index in range(N_GROUP):
        token_expert = expert_ids[group_index, :, 0].astype(jnp.int32)
        one_hot = (token_expert[:, None] == jnp.arange(EXPERTS, dtype=jnp.int32)[None, :]).astype(jnp.int32)
        one_hot = one_hot.reshape(N_EXPERT, TOK_DEV, EXPERTS)
        rank_all = jnp.cumsum(one_hot, axis=1) - one_hot
        rank_in = jnp.sum(rank_all * one_hot, axis=2)
        source = jnp.arange(N_EXPERT, dtype=jnp.int32)[:, None]
        slot_index = (token_expert.reshape(N_EXPERT, TOK_DEV) * buffer_rows + source * CAP + rank_in).reshape(-1).astype(jnp.int32)
        buffers = jnp.zeros((EXPERTS * buffer_rows, D), tokens.dtype).at[slot_index].set(tokens[group_index])
        combined = lax.map(expert_block, (buffers.reshape(EXPERTS, buffer_rows, D), per_expert))
        picked = combined.reshape(EXPERTS * buffer_rows, D)[slot_index]
        weighted = route_weight[group_index, :, 0][:, None] * picked
        outputs.append(weighted.astype(jnp.bfloat16))
    expert_out = jnp.stack(outputs, axis=0)
    return expert_out, new_outer, new_momentum
```

```python
import functools

import jax
import jax.numpy as jnp
from jax import lax
from jax.experimental import pallas as pl
from jax.experimental.pallas import tpu as pltpu
from jax.sharding import PartitionSpec as P

MESH = pl.DeviceIdType.MESH
F32 = jnp.float32
BF16 = jnp.bfloat16

outer_rate = 0.7
momentum_rate = 0.9

WIDTH = 4096
HALF = 2048
CAP = 32
PARTS = 4
PART = HALF // PARTS
BLOCK = 256
ORDER = (("g", 0), ("g", 1), ("d", 0), ("d", 1), ("g", 2), ("d", 2), ("d", 3))
STEPS = len(ORDER)
AHEAD = 2


def kernel(
    tok, ids, rw, inner, outer, mom, eo, no, nm,
    tokv, packed, xs, wg, wd, rg, rd, og, od, ob, mb, hs, hid, ys, ret, eov, place,
    s_rs, r_rs, s_ag, r_ag, l_in, l_out, s_sg, r_sg, s_dz, r_dz, s_df, r_df, s_sd, r_sd,
    s_dp, r_dp, s_xz, r_xz, s_xf, r_xf, s_h, r_h, s_rt, r_rt, l_rt, l_eo, l_tok,
):
    g = lax.axis_index("group")
    e = lax.axis_index("expert")
    low = lax.div(e, 32)
    y = lax.rem(lax.div(e, 8), 4)
    z = lax.rem(lax.div(e, 2), 4)
    c = lax.rem(e, 2)
    x = g * 2 + low

    def device(xx, yy, zz, cc):
        return (lax.div(xx, 2), ((lax.rem(xx, 2) * 4 + yy) * 4 + zz) * 2 + cc)

    def turn(a, n):
        return lax.rem(a + n, 4)

    partner = device(turn(x, 2), y, z, c)
    sibling = device(x, y, z, 1 - c)
    up, down, far = (device(x, y, turn(z, n), c) for n in (1, 3, 2))
    xn = (x, turn(x, 1), turn(x, 3))

    barrier = pltpu.get_barrier_semaphore()
    near = [partner, sibling, up, down, far]
    near += [device(x, turn(y, dy), z, c) for dy in (1, 2, 3)]
    near += [device(xn[s], turn(y, dy), z, c) for s in (1, 2) for dy in range(4)]
    for other in near:
        pl.semaphore_signal(barrier, inc=1, device_id=other, device_id_type=MESH)

    sends = []
    locals_ = []

    def send(src, dst, ss, rs, dev):
        copy = pltpu.make_async_remote_copy(
            src_ref=src, dst_ref=dst, send_sem=ss, recv_sem=rs, device_id=dev, device_id_type=MESH
        )
        copy.start()
        sends.append(copy)

    def arrived(dst, ss, rs):
        pltpu.make_async_remote_copy(
            src_ref=dst, dst_ref=dst, send_sem=ss, recv_sem=rs, device_id=sibling, device_id_type=MESH
        ).wait_recv()

    def local(src, dst, sem):
        copy = pltpu.make_async_copy(src, dst, sem)
        copy.start()
        return copy

    mine = pl.multiple_of(g * HALF, HALF)
    theirs = pl.multiple_of((1 - g) * HALF, HALF)
    half_of = (mine, theirs)

    def in_view(ref, step, offset):
        kind, n = ORDER[step]
        if kind == "g":
            return ref.at[0:2, n, :, pl.ds(offset, HALF)]
        return ref.at[2, :, :, pl.ds(offset + n * PART, PART)]

    def half_view(ref_g, ref_d, step):
        kind, n = ORDER[step]
        if kind == "g":
            return ref_g.at[n]
        return ref_d.at[:, :, pl.ds(n * PART, PART)]

    def wg_view(n, kind, core):
        return wg.at[n, :, core, :, pl.ds(half_of[kind], HALF)]

    def wd_view(n, kind, zz, core):
        return wd.at[zz, :, core, :, pl.ds(half_of[kind] + n * PART, PART)]

    def fresh_view(step, kind):
        name, n = ORDER[step]
        return wg_view(n, kind, c) if name == "g" else wd_view(n, kind, z, c)

    tok_copy = local(tok, tokv, l_tok)
    loads = []
    for step in range(STEPS):
        loads.append(
            (
                local(in_view(inner, step, mine), half_view(og, od, step), l_in.at[step, 0]),
                local(in_view(outer, step, 0), in_view(ob, step, 0), l_in.at[step, 1]),
                local(in_view(mom, step, 0), in_view(mb, step, 0), l_in.at[step, 2]),
            )
        )

    lane = lax.broadcasted_iota(jnp.int32, (128, 128), 1)
    row = lax.broadcasted_iota(jnp.int32, (128, 128), 0)
    named = ids[...]
    one_hot = (lane == named).astype(F32)
    earlier = (lane < row).astype(F32)
    rank = jnp.dot(earlier.astype(BF16), one_hot.astype(BF16), preferred_element_type=F32)
    rank = jnp.sum(rank * one_hot, axis=1, keepdims=True)
    slot = named.astype(F32) * CAP + rank
    wide = lax.broadcasted_iota(jnp.int32, (128, BLOCK), 1).astype(F32)
    placing = (wide == slot).astype(F32)
    place[...] = placing.astype(BF16)
    pack = jnp.transpose(placing).astype(BF16)
    tok_copy.wait()

    @pl.loop(0, WIDTH // 512)
    def _(n):
        cols = pl.ds(pl.multiple_of(n * 512, 512), 512)
        packed[:, cols] = jnp.dot(pack, tokv[:, cols], preferred_element_type=F32).astype(BF16)

    pl.semaphore_wait(barrier, len(near))

    def start_rs(step):
        if step < STEPS:
            send(
                in_view(inner, step, theirs), half_view(rg, rd, step),
                s_rs.at[step], r_rs.at[step], partner,
            )

    for step in range(AHEAD):
        start_rs(step)

    def rows_at(start, size):
        return pl.ds(pl.multiple_of(start, 16), size)

    def spread(n):
        if n < 3:
            return 0, n + 1, 0, 32
        if n < 7:
            return 1, n - 3, 0, 16
        return 2, n - 7, 16, 16

    def expert_rows(s, yy, first, size):
        owner = low if s == 0 else 1 - low
        return rows_at((owner * 4 + yy) * CAP + first, size)

    def buffer_rows(s, yy, first, size):
        return rows_at((0 if s == 0 else 128) + yy * 32 + first, size)

    xs[z, rows_at(y * 32, 32), :] = packed[expert_rows(0, y, 0, 32), :]
    for n in (0, 3, 7, 2, 4, 8, 6, 10, 1, 5, 9):
        s, dy, first, size = spread(n)
        send(
            packed.at[expert_rows(s, turn(y, dy), first, size)],
            xs.at[z, buffer_rows(s, y, first, size)],
            s_dp.at[n], r_dp.at[n], device(xn[s], turn(y, dy), z, c),
        )

    def x_piece(zz, p):
        s, dy = p // 4, p % 4
        return xs.at[zz, buffer_rows(s, turn(y, 4 - dy), 0, 32)]

    def dispatch(p):
        s, dy = p // 4, p % 4
        for n in ((dy - 1,) if s == 0 else (3 + dy, 7 + dy)):
            if n >= 0:
                sn, _, first, size = spread(n)
                arrived(
                    xs.at[z, buffer_rows(sn, turn(y, 4 - dy), first, size)], s_dp.at[n], r_dp.at[n]
                )
        view = x_piece(z, p)
        send(view, view, s_xz.at[p, 0], r_xz.at[p, 0], up)
        send(view, view, s_xz.at[p, 1], r_xz.at[p, 1], down)

    def x_forward(p):
        way = p // 4
        view = x_piece(turn(z, 1 if way else 3), p)
        arrived(view, s_xz.at[p, way], r_xz.at[p, way])
        send(view, view, s_xf.at[p], r_xf.at[p], down if way else up)

    def x_rest():
        for p in range(8):
            way = 1 - p // 4
            arrived(x_piece(turn(z, 1 if way else 3), p), s_xz.at[p, way], r_xz.at[p, way])
        for p in range(8):
            arrived(x_piece(turn(z, 2), p), s_xf.at[p], r_xf.at[p])

    def outer_step(o, m, a, b):
        pseudo = o - (a.astype(F32) + b.astype(F32)) / 2
        new_m = momentum_rate * m + pseudo
        return o - outer_rate * (pseudo + momentum_rate * new_m), new_m

    def share(step, kind):
        name, n = ORDER[step]
        view = fresh_view(step, kind)
        if name == "g":
            send(view, view, s_sg.at[n, kind], r_sg.at[n, kind], sibling)
        else:
            send(view, view, s_dz.at[n, kind, 0], r_dz.at[n, kind, 0], up)
            send(view, view, s_dz.at[n, kind, 1], r_dz.at[n, kind, 1], down)
            send(view, view, s_sd.at[n, kind, 0], r_sd.at[n, kind, 0], sibling)

    def update(step):
        name, n = ORDER[step]
        for copy in loads[step]:
            copy.wait()
        arrived(half_view(rg, rd, step), s_rs.at[step], r_rs.at[step])
        for i in range(2 if name == "g" else 3):

            @pl.loop(0, 4)
            def _(t):
                rows = pl.ds(pl.multiple_of(t * 16, 16), 16)
                if name == "g":
                    at = (i, n, rows, slice(None))
                    a, b = og[n, i, rows, :], rg[n, i, rows, :]
                else:
                    at = (2, i, rows, pl.ds(n * PART, PART))
                    a, b = od[i, rows, pl.ds(n * PART, PART)], rd[i, rows, pl.ds(n * PART, PART)]
                new_o, new_m = outer_step(ob[at], mb[at], a, b)
                ob[at] = new_o
                mb[at] = new_m
                if name == "g":
                    wg[n, i, c, rows, pl.ds(mine, HALF)] = new_o.astype(BF16)
                else:
                    wd[z, i, c, rows, pl.ds(mine + n * PART, PART)] = new_o.astype(BF16)

        view = fresh_view(step, 0)
        send(view, view, s_ag.at[step], r_ag.at[step], partner)
        start_rs(step + AHEAD)
        share(step, 0)
        locals_.append(local(in_view(ob, step, 0), in_view(no, step, 0), l_out.at[step, 0]))
        locals_.append(local(in_view(mb, step, 0), in_view(nm, step, 0), l_out.at[step, 1]))

    def gathered(step):
        arrived(fresh_view(step, 1), s_ag.at[step], r_ag.at[step])
        share(step, 1)

    def d_near(n, kind):
        for way in (0, 1):
            view = wd_view(n, kind, turn(z, 1 if way else 3), c)
            arrived(view, s_dz.at[n, kind, way], r_dz.at[n, kind, way])
            if way == kind:
                send(view, view, s_df.at[n, kind], r_df.at[n, kind], down if way else up)
            send(view, view, s_sd.at[n, kind, 1 + way], r_sd.at[n, kind, 1 + way], sibling)

    def d_far(n, kind):
        view = wd_view(n, kind, turn(z, 2), c)
        arrived(view, s_df.at[n, kind], r_df.at[n, kind])
        send(view, view, s_sd.at[n, kind, 3], r_sd.at[n, kind, 3], sibling)

    def hid_cols(zz, n):
        return pl.ds(pl.multiple_of((zz * 3 + n) * 128, 128), 128)

    def hidden(n):
        for kind in (0, 1):
            arrived(wg_view(n, kind, 1 - c), s_sg.at[n, kind], r_sg.at[n, kind])

        @pl.loop(0, 4)
        def _(r):
            zz = turn(z, r + 1)
            both = lax.dot_general(
                xs[zz], wg[n].reshape(256, WIDTH), (((1,), (1,)), ((), ())),
                preferred_element_type=F32,
            )
            gate = both[:, :128]
            value = (gate / (1.0 + jnp.exp(-gate)) * both[:, 128:]).astype(BF16)
            hs[n, r] = value

            @pl.when(r < 3)
            def _():
                pltpu.make_async_remote_copy(
                    src_ref=hs.at[n, r], dst_ref=hid.at[:, hid_cols(z, n)],
                    send_sem=s_h.at[n, r], recv_sem=r_h.at[n, r],
                    device_id=device(x, y, zz, c), device_id_type=MESH,
                ).start()

        hid[:, hid_cols(z, n)] = hs[n, 3]
        for r in range(3):
            sends.append(
                pltpu.make_async_remote_copy(
                    src_ref=hs.at[n, r], dst_ref=hid.at[:, hid_cols(z, n)],
                    send_sem=s_h.at[n, r], recv_sem=r_h.at[n, r],
                    device_id=device(x, y, turn(z, r + 1), c), device_id_type=MESH,
                )
            )

    def hidden_rest():
        for n in range(3):
            for r in range(3):
                arrived(hid.at[:, hid_cols(turn(z, 3 - r), n)], s_h.at[n, r], r_h.at[n, r])

    def project(n):
        for kind in (0, 1):
            for k, dz in enumerate((0, 3, 1, 2)):
                arrived(
                    wd_view(n, kind, turn(z, dz), 1 - c), s_sd.at[n, kind, k], r_sd.at[n, kind, k]
                )
        for h in (0, 1):

            @pl.loop(0, PART // 256)
            def _(t):
                cols = pl.ds(pl.multiple_of(n * PART + t * 256, 256), 256)
                wide_cols = pl.ds(pl.multiple_of(h * HALF + n * PART + t * 256, 256), 256)
                ys[h, :, cols] = jnp.dot(
                    hid[...], wd[:, :, :, :, wide_cols].reshape(1536, 256),
                    preferred_element_type=F32,
                ).astype(BF16)

        cols = pl.ds(n * PART, PART)
        for m in range(11):
            s, dy, first, size = spread(m)
            back = xn[(0, 2, 1)[s]]
            send(
                ys.at[:, buffer_rows(s, turn(y, 4 - dy), first, size), cols],
                ret.at[:, rows_at((low * 4 + y) * CAP + first, size), cols],
                s_rt.at[n, m], r_rt.at[n, m], device(back, turn(y, 4 - dy), z, c),
            )
        ret[:, expert_rows(0, y, 0, 32), cols] = ys[:, buffer_rows(0, y, 0, 32), cols]

    def finish(n):
        cols = pl.ds(n * PART, PART)
        for m in range(11):
            s, dy, first, size = spread(m)
            arrived(
                ret.at[:, expert_rows(s, turn(y, dy), first, size), cols],
                s_rt.at[n, m], r_rt.at[n, m],
            )
        for h in (0, 1):
            picked = jnp.dot(place[...], ret[h, :, cols], preferred_element_type=F32)
            wide_cols = pl.ds(h * HALF + n * PART, PART)
            eov[:, wide_cols] = (rw[...] * picked).astype(BF16)
            locals_.append(local(eov.at[:, wide_cols], eo.at[:, wide_cols], l_eo.at[n, h]))

    dispatch(0)
    for p in (1, 4, 5, 3):
        dispatch(p)
    update(0)
    for p in (7, 2, 6):
        dispatch(p)
    x_forward(0)
    x_forward(1)
    x_forward(4)
    update(1)
    x_forward(5)
    x_forward(3)
    gathered(0)
    update(2)
    x_forward(7)
    x_forward(2)
    x_forward(6)
    gathered(1)
    update(3)
    gathered(2)
    x_rest()
    hidden(0)
    update(4)
    gathered(3)
    hidden(1)
    update(5)
    d_near(0, 0)
    d_near(0, 1)
    gathered(4)
    d_far(0, 0)
    d_far(0, 1)
    d_near(1, 0)
    d_near(1, 1)
    hidden(2)
    update(6)
    gathered(5)
    d_far(1, 0)
    d_far(1, 1)
    gathered(6)
    hidden_rest()
    project(0)
    d_near(2, 0)
    d_near(2, 1)
    project(1)
    d_far(2, 0)
    d_far(2, 1)
    d_near(3, 0)
    d_near(3, 1)
    project(2)
    finish(0)
    d_far(3, 0)
    d_far(3, 1)
    finish(1)
    project(3)
    finish(2)
    finish(3)

    for copy in sends:
        copy.wait_send()
    for copy in locals_:
        copy.wait()


def per_device(tokens, expert_ids, route_weight, inner_weights, outer_weights, momentum):
    dma = pltpu.SemaphoreType.DMA
    vmem = pltpu.VMEM
    any_space = pl.BlockSpec(memory_space=pl.ANY)
    in_vmem = pl.BlockSpec(memory_space=pltpu.VMEM)
    weights = (3, 3, 64, HALF)
    scratch = [
        vmem((128, WIDTH), BF16),
        vmem((BLOCK, WIDTH), BF16),
        vmem((4, BLOCK, WIDTH), BF16),
        vmem((3, 2, 2, 64, WIDTH), BF16),
        vmem((4, 3, 2, 64, WIDTH), BF16),
        vmem((3, 2, 64, HALF), BF16),
        vmem((3, 64, HALF), BF16),
        vmem((3, 2, 64, HALF), BF16),
        vmem((3, 64, HALF), BF16),
        vmem(weights, F32),
        vmem(weights, F32),
        vmem((3, 4, BLOCK, 128), BF16),
        vmem((BLOCK, 1536), BF16),
        vmem((2, BLOCK, HALF), BF16),
        vmem((2, BLOCK, HALF), BF16),
        vmem((128, WIDTH), BF16),
        vmem((128, BLOCK), BF16),
    ]
    scratch += [dma((STEPS,))] * 4
    scratch += [dma((STEPS, 3)), dma((STEPS, 2))]
    scratch += [dma((3, 2))] * 2
    scratch += [dma((PARTS, 2, 2))] * 2
    scratch += [dma((PARTS, 2))] * 2
    scratch += [dma((PARTS, 2, 4))] * 2
    scratch += [dma((11,))] * 2
    scratch += [dma((8, 2))] * 2
    scratch += [dma((8,))] * 2
    scratch += [dma((3, 3))] * 2
    scratch += [dma((PARTS, 11))] * 2
    scratch += [dma((1,)), dma((PARTS, 2)), dma]
    out, new_outer, new_momentum = pl.pallas_call(
        kernel,
        out_shape=(
            jax.ShapeDtypeStruct((128, WIDTH), BF16),
            jax.ShapeDtypeStruct(weights, F32),
            jax.ShapeDtypeStruct(weights, F32),
        ),
        in_specs=[any_space, in_vmem, in_vmem, any_space, any_space, any_space],
        out_specs=(any_space,) * 3,
        scratch_shapes=scratch,
        compiler_params=pltpu.CompilerParams(
            collective_id=0, has_side_effects=True, vmem_limit_bytes=62 << 20
        ),
    )(
        tokens.reshape(128, WIDTH),
        expert_ids.reshape(128, 1),
        route_weight.reshape(128, 1),
        inner_weights.reshape(3, 3, 64, WIDTH),
        outer_weights.reshape(weights),
        momentum.reshape(weights),
    )
    full = (3, 192, HALF)
    return out[None], new_outer.reshape(full), new_momentum.reshape(full)


def solution(mesh):
    in_specs = (
        P("group", "expert", None),
        P("group", "expert", None),
        P("group", "expert", None),
        P("group", None, "expert", None),
        P(None, "expert", "group"),
        P(None, "expert", "group"),
    )
    out_specs = (P("group", "expert", None), P(None, "expert", "group"), P(None, "expert", "group"))
    return jax.shard_map(
        per_device, mesh=mesh, in_specs=in_specs, out_specs=out_specs, check_vma=False
    )
```

```python
import functools

import jax
import jax.numpy as jnp
from jax import lax
from jax.experimental import pallas as pl
from jax.experimental.pallas import tpu as pltpu
from jax.sharding import PartitionSpec as P

MESH = pl.DeviceIdType.MESH
F32 = jnp.float32
BF16 = jnp.bfloat16

outer_rate = 0.7
momentum_rate = 0.9

WIDTH = 4096
HALF = 2048
CAP = 32
PARTS = 4
PART = HALF // PARTS
BLOCK = 256
GATES = 3
STEPS = [("g", n) for n in range(GATES)] + [("d", n) for n in range(PARTS)]

SCHEDULE = (
    ("start_rs", "d", 2),
    ("start_rs", "d", 1),
    ("pack",),
    ("scatter", 1),
    ("dispatch", 0),
    ("scatter", 4),
    ("scatter", 7),
    ("scatter", 8),
    ("start_rs", "g", 2),
    ("scatter", 2),
    ("scatter", 3),
    ("scatter", 10),
    ("update", "d", 2),
    ("dispatch", 2),
    ("start_rs", "d", 0),
    ("scatter", 0),
    ("dispatch", 5),
    ("dispatch", 1),
    ("scatter", 9),
    ("dispatch", 4),
    ("scatter", 5),
    ("start_rs", "g", 1),
    ("x_forward", 1),
    ("d_send", 2, 0),
    ("update", "d", 1),
    ("scatter", 6),
    ("x_forward", 2),
    ("dispatch", 3),
    ("update", "g", 2),
    ("gathered", "d", 2),
    ("start_rs", "g", 0),
    ("dispatch", 6),
    ("d_send", 2, 1),
    ("d_send", 1, 0),
    ("dispatch", 7),
    ("x_forward", 4),
    ("x_forward", 0),
    ("d_near", 2, 1, 1),
    ("start_rs", "d", 3),
    ("gathered", "d", 1),
    ("x_forward", 6),
    ("x_forward", 3),
    ("d_far", 2, 1),
    ("x_forward", 5),
    ("update", "g", 1),
    ("update", "d", 0),
    ("d_send", 1, 1),
    ("update", "g", 0),
    ("d_near", 2, 0, 0),
    ("x_forward", 7),
    ("d_send", 0, 0),
    ("gathered", "g", 2),
    ("d_near", 1, 1, 1),
    ("d_far", 2, 0),
    ("d_near", 1, 0, 0),
    ("d_near", 2, 0, 1),
    ("d_near", 1, 0, 1),
    ("gathered", "g", 1),
    ("update", "d", 3),
    ("d_near", 1, 1, 0),
    ("gathered", "d", 0),
    ("x_rest",),
    ("d_send", 3, 0),
    ("d_send", 0, 1),
    ("hidden", 2),
    ("d_near", 2, 1, 0),
    ("d_far", 1, 1),
    ("d_far", 1, 0),
    ("hidden", 1),
    ("gathered", "g", 0),
    ("d_near", 0, 0, 1),
    ("hidden", 0),
    ("d_near", 0, 0, 0),
    ("gathered", "d", 3),
    ("d_near", 0, 1, 0),
    ("d_send", 3, 1),
    ("d_near", 0, 1, 1),
    ("hidden_rest",),
    ("project", 2),
    ("project", 1),
    ("d_far", 0, 0),
    ("d_near", 3, 1, 1),
    ("d_near", 3, 0, 0),
    ("d_far", 0, 1),
    ("d_near", 3, 0, 1),
    ("d_near", 3, 1, 0),
    ("project", 0),
    ("d_far", 3, 0),
    ("d_far", 3, 1),
    ("project", 3),
    ("finish", 0),
    ("finish", 1),
    ("finish", 2),
    ("finish", 3),
)


def kernel(
    tok, ids, rw, inner, outer, mom, eov, ob, mb,
    tokv, packed, xs, wg, wd, rg, rd, og, od, hs, hid, ys, ret, place, weight,
    s_rs, r_rs, s_ag, r_ag, l_in, s_sg, r_sg, s_dz, r_dz, s_df, r_df, s_sd, r_sd,
    s_dp, r_dp, s_xz, r_xz, s_xf, r_xf, s_h, r_h, s_rt, r_rt, l_tok,
):
    g = lax.axis_index("group")
    e = lax.axis_index("expert")
    low = lax.div(e, 32)
    y = lax.rem(lax.div(e, 8), 4)
    z = lax.rem(lax.div(e, 2), 4)
    c = lax.rem(e, 2)
    x = g * 2 + low

    def device(xx, yy, zz, cc):
        return (lax.div(xx, 2), ((lax.rem(xx, 2) * 4 + yy) * 4 + zz) * 2 + cc)

    def turn(a, n):
        return lax.rem(a + n, 4)

    partner = device(turn(x, 2), y, z, c)
    sibling = device(x, y, z, 1 - c)
    up, down, far = (device(x, y, turn(z, n), c) for n in (1, 3, 2))
    xn = (x, turn(x, 1), turn(x, 3))

    barrier = pltpu.get_barrier_semaphore()
    near = [partner, sibling, up, down, far]
    near += [device(x, turn(y, dy), z, c) for dy in (1, 2, 3)]
    near += [device(xn[s], turn(y, dy), z, c) for s in (1, 2) for dy in range(4)]
    for other in near:
        pl.semaphore_signal(barrier, inc=1, device_id=other, device_id_type=MESH)

    sends = []

    def send(src, dst, ss, rs, dev):
        copy = pltpu.make_async_remote_copy(
            src_ref=src, dst_ref=dst, send_sem=ss, recv_sem=rs, device_id=dev, device_id_type=MESH
        )
        copy.start()
        sends.append(copy)

    def arrived(dst, ss, rs):
        pltpu.make_async_remote_copy(
            src_ref=dst, dst_ref=dst, send_sem=ss, recv_sem=rs, device_id=sibling, device_id_type=MESH
        ).wait_recv()

    def local(src, dst, sem):
        copy = pltpu.make_async_copy(src, dst, sem)
        copy.start()
        return copy

    mine = pl.multiple_of(g * HALF, HALF)
    theirs = pl.multiple_of((1 - g) * HALF, HALF)
    half_of = (mine, theirs)

    def in_view(ref, step, offset):
        kind, n = STEPS[step]
        if kind == "g":
            return ref.at[0:2, n, :, pl.ds(offset, HALF)]
        return ref.at[2, :, :, pl.ds(offset + n * PART, PART)]

    def half_view(ref_g, ref_d, step):
        kind, n = STEPS[step]
        if kind == "g":
            return ref_g.at[n]
        return ref_d.at[:, :, pl.ds(n * PART, PART)]

    def wg_view(n, kind, core):
        return wg.at[n, :, core, :, pl.ds(half_of[kind], HALF)]

    def wd_view(n, kind, zz, core):
        return wd.at[zz, :, core, :, pl.ds(half_of[kind] + n * PART, PART)]

    def fresh_view(step, kind):
        name, n = STEPS[step]
        return wg_view(n, kind, c) if name == "g" else wd_view(n, kind, z, c)

    tok_copy = local(tok, tokv, l_tok)
    loads = []
    for step in range(len(STEPS)):
        loads.append(
            (
                local(in_view(inner, step, mine), half_view(og, od, step), l_in.at[step, 0]),
                local(in_view(outer, step, 0), in_view(ob, step, 0), l_in.at[step, 1]),
                local(in_view(mom, step, 0), in_view(mb, step, 0), l_in.at[step, 2]),
            )
        )

    def pack():
        lane = lax.broadcasted_iota(jnp.int32, (128, 128), 1)
        row = lax.broadcasted_iota(jnp.int32, (128, 128), 0)
        named = ids[...]
        one_hot = (row == named).astype(F32)
        earlier = (row < lane).astype(BF16)
        rank = jnp.dot(one_hot.astype(BF16), earlier, preferred_element_type=F32)
        rank = jnp.sum(rank * one_hot, axis=0, keepdims=True)
        slot = named.astype(F32) * CAP + rank
        tall = lax.broadcasted_iota(jnp.int32, (BLOCK, 128), 0).astype(F32)
        placing = (tall == slot).astype(F32)
        place[...] = jnp.transpose(placing).astype(BF16)
        weight[...] = jnp.sum(jnp.where(lane == row, rw[...], 0.0), axis=1, keepdims=True)
        tok_copy.wait()

        @pl.loop(0, WIDTH // 512)
        def _(n):
            cols = pl.ds(pl.multiple_of(n * 512, 512), 512)
            packed[:, cols] = jnp.dot(
                placing.astype(BF16), tokv[:, cols], preferred_element_type=F32
            ).astype(BF16)

        xs[z, rows_at(y * 32, 32), :] = packed[expert_rows(0, y, 0, 32), :]

    def start_rs(name, n):
        step = STEPS.index((name, n))
        send(
            in_view(inner, step, theirs), half_view(rg, rd, step),
            s_rs.at[step], r_rs.at[step], partner,
        )

    def rows_at(start, size):
        return pl.ds(pl.multiple_of(start, 16), size)

    def spread(n):
        if n < 3:
            return 0, n + 1, 0, 32
        if n < 7:
            return 1, n - 3, 0, 16
        return 2, n - 7, 16, 16

    def expert_rows(s, yy, first, size):
        owner = low if s == 0 else 1 - low
        return rows_at((owner * 4 + yy) * CAP + first, size)

    def buffer_rows(s, yy, first, size):
        return rows_at((0 if s == 0 else 128) + yy * 32 + first, size)

    def scatter(n):
        s, dy, first, size = spread(n)
        send(
            packed.at[expert_rows(s, turn(y, dy), first, size)],
            xs.at[z, buffer_rows(s, y, first, size)],
            s_dp.at[n], r_dp.at[n], device(xn[s], turn(y, dy), z, c),
        )

    def x_piece(zz, p):
        s, dy = p // 4, p % 4
        return xs.at[zz, buffer_rows(s, turn(y, 4 - dy), 0, 32)]

    def dispatch(p):
        s, dy = p // 4, p % 4
        for n in ((dy - 1,) if s == 0 else (3 + dy, 7 + dy)):
            if n >= 0:
                sn, _, first, size = spread(n)
                arrived(
                    xs.at[z, buffer_rows(sn, turn(y, 4 - dy), first, size)], s_dp.at[n], r_dp.at[n]
                )
        view = x_piece(z, p)
        send(view, view, s_xz.at[p, 0], r_xz.at[p, 0], up)
        send(view, view, s_xz.at[p, 1], r_xz.at[p, 1], down)

    def x_forward(p):
        way = p // 4
        view = x_piece(turn(z, 1 if way else 3), p)
        arrived(view, s_xz.at[p, way], r_xz.at[p, way])
        send(view, view, s_xf.at[p], r_xf.at[p], down if way else up)

    def x_rest():
        for p in range(8):
            way = 1 - p // 4
            arrived(x_piece(turn(z, 1 if way else 3), p), s_xz.at[p, way], r_xz.at[p, way])
        for p in range(8):
            arrived(x_piece(turn(z, 2), p), s_xf.at[p], r_xf.at[p])

    def outer_step(o, m, a, b):
        pseudo = o - (a.astype(F32) + b.astype(F32)) / 2
        new_m = momentum_rate * m + pseudo
        return o - outer_rate * (pseudo + momentum_rate * new_m), new_m

    def share(name, n, kind):
        step = STEPS.index((name, n))
        view = fresh_view(step, kind)
        if name == "g":
            send(view, view, s_sg.at[n, kind], r_sg.at[n, kind], sibling)
        else:
            send(view, view, s_sd.at[n, kind, 0], r_sd.at[n, kind, 0], sibling)

    def d_send(n, kind):
        view = wd_view(n, kind, z, c)
        send(view, view, s_dz.at[n, kind, 0], r_dz.at[n, kind, 0], up)
        send(view, view, s_dz.at[n, kind, 1], r_dz.at[n, kind, 1], down)

    def update(name, n):
        step = STEPS.index((name, n))
        for copy in loads[step]:
            copy.wait()
        arrived(half_view(rg, rd, step), s_rs.at[step], r_rs.at[step])
        for i in range(2 if name == "g" else 3):

            @pl.loop(0, 4)
            def _(t):
                rows = pl.ds(pl.multiple_of(t * 16, 16), 16)
                if name == "g":
                    at = (i, n, rows, slice(None))
                    a, b = og[n, i, rows, :], rg[n, i, rows, :]
                else:
                    at = (2, i, rows, pl.ds(n * PART, PART))
                    a, b = od[i, rows, pl.ds(n * PART, PART)], rd[i, rows, pl.ds(n * PART, PART)]
                new_o, new_m = outer_step(ob[at], mb[at], a, b)
                ob[at] = new_o
                mb[at] = new_m
                if name == "g":
                    wg[n, i, c, rows, pl.ds(mine, HALF)] = new_o.astype(BF16)
                else:
                    wd[z, i, c, rows, pl.ds(mine + n * PART, PART)] = new_o.astype(BF16)

        view = fresh_view(step, 0)
        send(view, view, s_ag.at[step], r_ag.at[step], partner)
        share(name, n, 0)

    def gathered(name, n):
        step = STEPS.index((name, n))
        arrived(fresh_view(step, 1), s_ag.at[step], r_ag.at[step])
        share(name, n, 1)

    def d_near(n, kind, way):
        view = wd_view(n, kind, turn(z, 1 if way else 3), c)
        arrived(view, s_dz.at[n, kind, way], r_dz.at[n, kind, way])
        if way == kind:
            send(view, view, s_df.at[n, kind], r_df.at[n, kind], down if way else up)
        send(view, view, s_sd.at[n, kind, 1 + way], r_sd.at[n, kind, 1 + way], sibling)

    def d_far(n, kind):
        view = wd_view(n, kind, turn(z, 2), c)
        arrived(view, s_df.at[n, kind], r_df.at[n, kind])
        send(view, view, s_sd.at[n, kind, 3], r_sd.at[n, kind, 3], sibling)

    def hid_cols(zz, n):
        return pl.ds(pl.multiple_of((zz * 3 + n) * 128, 128), 128)

    def hidden(n):
        for kind in (0, 1):
            arrived(wg_view(n, kind, 1 - c), s_sg.at[n, kind], r_sg.at[n, kind])

        @pl.loop(0, 4)
        def _(r):
            zz = turn(z, r + 1)
            both = lax.dot_general(
                xs[zz], wg[n].reshape(256, WIDTH), (((1,), (1,)), ((), ())),
                preferred_element_type=F32,
            )
            gate = both[:, :128]
            value = (gate / (1.0 + jnp.exp(-gate)) * both[:, 128:]).astype(BF16)
            hs[n, r] = value

            @pl.when(r < 3)
            def _():
                pltpu.make_async_remote_copy(
                    src_ref=hs.at[n, r], dst_ref=hid.at[:, hid_cols(z, n)],
                    send_sem=s_h.at[n, r], recv_sem=r_h.at[n, r],
                    device_id=device(x, y, zz, c), device_id_type=MESH,
                ).start()

        hid[:, hid_cols(z, n)] = hs[n, 3]
        for r in range(3):
            sends.append(
                pltpu.make_async_remote_copy(
                    src_ref=hs.at[n, r], dst_ref=hid.at[:, hid_cols(z, n)],
                    send_sem=s_h.at[n, r], recv_sem=r_h.at[n, r],
                    device_id=device(x, y, turn(z, r + 1), c), device_id_type=MESH,
                )
            )

    def hidden_rest():
        for n in range(3):
            for r in range(3):
                arrived(hid.at[:, hid_cols(turn(z, 3 - r), n)], s_h.at[n, r], r_h.at[n, r])

    def project(n):
        for kind in (0, 1):
            for k, dz in enumerate((0, 3, 1, 2)):
                arrived(
                    wd_view(n, kind, turn(z, dz), 1 - c), s_sd.at[n, kind, k], r_sd.at[n, kind, k]
                )
        for h in (0, 1):

            @pl.loop(0, PART // 256)
            def _(t):
                cols = pl.ds(pl.multiple_of(n * PART + t * 256, 256), 256)
                wide_cols = pl.ds(pl.multiple_of(h * HALF + n * PART + t * 256, 256), 256)
                ys[h, :, cols] = jnp.dot(
                    hid[...], wd[:, :, :, :, wide_cols].reshape(1536, 256),
                    preferred_element_type=F32,
                ).astype(BF16)

        cols = pl.ds(n * PART, PART)
        for m in (0, 3, 7, 2, 4, 8, 6, 10, 1, 5, 9):
            s, dy, first, size = spread(m)
            back = xn[(0, 2, 1)[s]]
            send(
                ys.at[:, buffer_rows(s, turn(y, 4 - dy), first, size), cols],
                ret.at[:, rows_at((low * 4 + y) * CAP + first, size), cols],
                s_rt.at[n, m], r_rt.at[n, m], device(back, turn(y, 4 - dy), z, c),
            )
        ret[:, expert_rows(0, y, 0, 32), cols] = ys[:, buffer_rows(0, y, 0, 32), cols]

    def finish(n):
        cols = pl.ds(n * PART, PART)
        for m in range(11):
            s, dy, first, size = spread(m)
            arrived(
                ret.at[:, expert_rows(s, turn(y, dy), first, size), cols],
                s_rt.at[n, m], r_rt.at[n, m],
            )
        for h in (0, 1):
            picked = jnp.dot(place[...], ret[h, :, cols], preferred_element_type=F32)
            wide_cols = pl.ds(h * HALF + n * PART, PART)
            eov[:, wide_cols] = (weight[...] * picked).astype(BF16)

    pl.semaphore_wait(barrier, len(near))
    actions = (
        pack, start_rs, scatter, dispatch, x_forward, x_rest, update, gathered, d_send, d_near,
        d_far, hidden, hidden_rest, project, finish,
    )
    actions = {action.__name__: action for action in actions}
    for name, *parts in SCHEDULE:
        actions[name](*parts)

    for copy in sends:
        copy.wait_send()


def per_device(tokens, expert_ids, route_weight, inner_weights, outer_weights, momentum):
    dma = pltpu.SemaphoreType.DMA
    vmem = pltpu.VMEM
    any_space = pl.BlockSpec(memory_space=pl.ANY)
    in_vmem = pl.BlockSpec(memory_space=pltpu.VMEM)
    weights = (3, 3, 64, HALF)
    scratch = [
        vmem((128, WIDTH), BF16),
        vmem((BLOCK, WIDTH), BF16),
        vmem((4, BLOCK, WIDTH), BF16),
        vmem((3, 2, 2, 64, WIDTH), BF16),
        vmem((4, 3, 2, 64, WIDTH), BF16),
        vmem((3, 2, 64, HALF), BF16),
        vmem((3, 64, HALF), BF16),
        vmem((3, 2, 64, HALF), BF16),
        vmem((3, 64, HALF), BF16),
        vmem((3, 4, BLOCK, 128), BF16),
        vmem((BLOCK, 1536), BF16),
        vmem((2, BLOCK, HALF), BF16),
        vmem((2, BLOCK, HALF), BF16),
        vmem((128, BLOCK), BF16),
        vmem((128, 1), F32),
    ]
    scratch += [dma((len(STEPS),))] * 4
    scratch += [dma((len(STEPS), 3))]
    scratch += [dma((3, 2))] * 2
    scratch += [dma((PARTS, 2, 2))] * 2
    scratch += [dma((PARTS, 2))] * 2
    scratch += [dma((PARTS, 2, 4))] * 2
    scratch += [dma((11,))] * 2
    scratch += [dma((8, 2))] * 2
    scratch += [dma((8,))] * 2
    scratch += [dma((3, 3))] * 2
    scratch += [dma((PARTS, 11))] * 2
    scratch += [dma]
    out, new_outer, new_momentum = pl.pallas_call(
        kernel,
        out_shape=(
            vmem((128, WIDTH), BF16),
            vmem(weights, F32),
            vmem(weights, F32),
        ),
        in_specs=[any_space, in_vmem, in_vmem, any_space, any_space, any_space],
        out_specs=(in_vmem,) * 3,
        scratch_shapes=scratch,
        compiler_params=pltpu.CompilerParams(
            collective_id=0, has_side_effects=True, vmem_limit_bytes=49 << 20
        ),
    )(
        tokens.reshape(128, WIDTH),
        expert_ids.reshape(1, 128),
        route_weight.reshape(1, 128),
        inner_weights.reshape(3, 3, 64, WIDTH),
        outer_weights.reshape(weights),
        momentum.reshape(weights),
    )
    full = (3, 192, HALF)
    return out[None], new_outer.reshape(full), new_momentum.reshape(full)


def solution(mesh):
    in_specs = (
        P("group", "expert", None),
        P("group", "expert", None),
        P("group", "expert", None),
        P("group", None, "expert", None),
        P(None, "expert", "group"),
        P(None, "expert", "group"),
    )
    out_specs = (P("group", "expert", None), P(None, "expert", "group"), P(None, "expert", "group"))
    return jax.shard_map(
        per_device, mesh=mesh, in_specs=in_specs, out_specs=out_specs, check_vma=False
    )
```

```python
import functools

import jax
import jax.numpy as jnp
from jax import lax
from jax.experimental import pallas as pl
from jax.experimental.pallas import tpu as pltpu
from jax.sharding import PartitionSpec as P

MESH = pl.DeviceIdType.MESH
F32 = jnp.float32
BF16 = jnp.bfloat16

outer_rate = 0.7
momentum_rate = 0.9

WIDTH = 4096
HALF = 2048
CAP = 32
WIDTHS = (512, 512, 512, 512)
PARTS = len(WIDTHS)
STARTS = [sum(WIDTHS[:n]) for n in range(PARTS)]
BLOCK = 256
GATES = 3
STEPS = [("g", n) for n in range(GATES)] + [("d", n) for n in range(PARTS)]

SCHEDULE = (
    ("start_rs", "d", 1),
    ("dispatch", 0),
    ("scatter", 0),
    ("start_rs", "d", 0),
    ("start_rs", "d", 3),
    ("scatter", 7),
    ("scatter", 2),
    ("update", "d", 1),
    ("d_send", 1, 0),
    ("update", "d", 0),
    ("d_send", 0, 0),
    ("dispatch", 1),
    ("dispatch", 3),
    ("scatter", 3),
    ("gathered", "d", 1),
    ("gathered", "d", 0),
    ("scatter", 4),
    ("scatter", 8),
    ("dispatch", 4),
    ("scatter", 10),
    ("d_near", 1, 0, 1),
    ("d_send", 1, 1),
    ("update", "d", 3),
    ("d_send", 0, 1),
    ("scatter", 6),
    ("scatter", 9),
    ("d_send", 3, 0),
    ("start_rs", "g", 0),
    ("dispatch", 5),
    ("scatter", 1),
    ("d_near", 0, 0, 0),
    ("x_forward", 4),
    ("x_forward", 3),
    ("dispatch", 2),
    ("start_rs", "g", 1),
    ("d_near", 0, 1, 1),
    ("dispatch", 7),
    ("scatter", 5),
    ("x_forward", 0),
    ("update", "g", 0),
    ("gathered", "d", 3),
    ("x_forward", 5),
    ("dispatch", 6),
    ("d_near", 0, 0, 1),
    ("start_rs", "g", 2),
    ("x_forward", 1),
    ("update", "g", 1),
    ("gathered", "g", 0),
    ("d_send", 3, 1),
    ("x_forward", 2),
    ("d_near", 1, 0, 0),
    ("d_near", 3, 0, 1),
    ("d_near", 3, 0, 0),
    ("x_forward", 7),
    ("x_forward", 6),
    ("update", "g", 2),
    ("d_far", 0, 1),
    ("d_near", 3, 1, 1),
    ("gathered", "g", 1),
    ("d_near", 1, 1, 1),
    ("x_rest",),
    ("d_far", 0, 0),
    ("hidden", 0),
    ("hidden", 1),
    ("gathered", "g", 2),
    ("start_rs", "d", 2),
    ("d_far", 1, 0),
    ("d_near", 3, 1, 0),
    ("d_near", 0, 1, 0),
    ("d_far", 1, 1),
    ("hidden", 2),
    ("update", "d", 2),
    ("d_send", 2, 0),
    ("hidden_rest",),
    ("project", 0),
    ("gathered", "d", 2),
    ("d_near", 1, 1, 0),
    ("d_far", 3, 0),
    ("d_send", 2, 1),
    ("d_near", 2, 0, 0),
    ("d_far", 3, 1),
    ("project", 1),
    ("d_near", 2, 1, 1),
    ("project", 3),
    ("d_near", 2, 0, 1),
    ("d_near", 2, 1, 0),
    ("d_far", 2, 0),
    ("d_far", 2, 1),
    ("project", 2),
    ("finish", 3),
    ("finish", 1),
    ("finish", 0),
    ("finish", 2),
)


def kernel(
    tok, ids, rw, inner, outer, mom, eov, ob, mb,
    tokv, packed, xs, wg, wd, rg, rd, og, od, hs, hid, ys, ret, place, weight,
    s_rs, r_rs, s_ag, r_ag, l_in, s_sg, r_sg, s_dz, r_dz, s_df, r_df, s_sd, r_sd,
    s_dp, r_dp, s_xz, r_xz, s_xf, r_xf, s_h, r_h, s_rt, r_rt, l_tok,
):
    g = lax.axis_index("group")
    e = lax.axis_index("expert")
    low = lax.div(e, 32)
    y = lax.rem(lax.div(e, 8), 4)
    z = lax.rem(lax.div(e, 2), 4)
    c = lax.rem(e, 2)
    x = g * 2 + low

    def device(xx, yy, zz, cc):
        return (lax.div(xx, 2), ((lax.rem(xx, 2) * 4 + yy) * 4 + zz) * 2 + cc)

    def turn(a, n):
        return lax.rem(a + n, 4)

    def around(a):
        way = 1 + 2 * lax.rem(a, 2)
        return a, turn(a, way), turn(a, 2), turn(a, 4 - way)

    ring, yn, zn = around(x), around(y), around(z)
    xn = (ring[0], ring[1], ring[3])
    partner = device(ring[2], y, z, c)
    sibling = device(x, y, z, 1 - c)
    zdev = [device(x, y, zz, c) for zz in zn]

    barrier = pltpu.get_barrier_semaphore()
    near = [partner, sibling] + zdev[1:]
    near += [device(x, yn[k], z, c) for k in (1, 2, 3)]
    near += [device(xn[s], yn[k], z, c) for s in (1, 2) for k in range(4)]
    for other in near:
        pl.semaphore_signal(barrier, inc=1, device_id=other, device_id_type=MESH)

    sends = []

    def send(src, dst, ss, rs, dev):
        copy = pltpu.make_async_remote_copy(
            src_ref=src, dst_ref=dst, send_sem=ss, recv_sem=rs, device_id=dev, device_id_type=MESH
        )
        copy.start()
        sends.append(copy)

    def arrived(dst, ss, rs):
        pltpu.make_async_remote_copy(
            src_ref=dst, dst_ref=dst, send_sem=ss, recv_sem=rs, device_id=sibling, device_id_type=MESH
        ).wait_recv()

    def local(src, dst, sem):
        copy = pltpu.make_async_copy(src, dst, sem)
        copy.start()
        return copy

    mine = pl.multiple_of(g * HALF, HALF)
    theirs = pl.multiple_of((1 - g) * HALF, HALF)
    half_of = (mine, theirs)

    def in_view(ref, step, offset):
        kind, n = STEPS[step]
        if kind == "g":
            return ref.at[0:2, n, :, pl.ds(offset, HALF)]
        return ref.at[2, :, :, pl.ds(offset + STARTS[n], WIDTHS[n])]

    def half_view(ref_g, ref_d, step):
        kind, n = STEPS[step]
        if kind == "g":
            return ref_g.at[n]
        return ref_d.at[:, :, pl.ds(STARTS[n], WIDTHS[n])]

    def wg_view(n, kind, core):
        return wg.at[n, :, core, :, pl.ds(half_of[kind], HALF)]

    def wd_view(n, kind, zz, core):
        return wd.at[zz, :, core, :, pl.ds(half_of[kind] + STARTS[n], WIDTHS[n])]

    def fresh_view(step, kind):
        name, n = STEPS[step]
        return wg_view(n, kind, c) if name == "g" else wd_view(n, kind, z, c)

    tok_copy = local(tok, tokv, l_tok)
    loads = {}
    for name, *part in SCHEDULE:
        if name == "update":
            step = STEPS.index(tuple(part))
            loads[step] = (
                local(in_view(inner, step, mine), half_view(og, od, step), l_in.at[step, 0]),
                local(in_view(outer, step, 0), in_view(ob, step, 0), l_in.at[step, 1]),
                local(in_view(mom, step, 0), in_view(mb, step, 0), l_in.at[step, 2]),
            )

    def pack():
        lane = lax.broadcasted_iota(jnp.int32, (128, 128), 1)
        row = lax.broadcasted_iota(jnp.int32, (128, 128), 0)
        named = ids[...]
        one_hot = (row == named).astype(F32)
        earlier = (row < lane).astype(BF16)
        rank = jnp.dot(one_hot.astype(BF16), earlier, preferred_element_type=F32)
        rank = jnp.sum(rank * one_hot, axis=0, keepdims=True)
        slot = named.astype(F32) * CAP + rank
        tall = lax.broadcasted_iota(jnp.int32, (BLOCK, 128), 0).astype(F32)
        placing = (tall == slot).astype(F32)
        place[...] = jnp.transpose(placing).astype(BF16)
        weight[...] = jnp.sum(jnp.where(lane == row, rw[...], 0.0), axis=1, keepdims=True)
        tok_copy.wait()

        @pl.loop(0, WIDTH // 512)
        def _(n):
            cols = pl.ds(pl.multiple_of(n * 512, 512), 512)
            packed[:, cols] = jnp.dot(
                placing.astype(BF16), tokv[:, cols], preferred_element_type=F32
            ).astype(BF16)

        xs[z, rows_at(y * 32, 32), :] = packed[expert_rows(0, y, 0, 32), :]

    def start_rs(name, n):
        step = STEPS.index((name, n))
        send(
            in_view(inner, step, theirs), half_view(rg, rd, step),
            s_rs.at[step], r_rs.at[step], partner,
        )

    def rows_at(start, size):
        return pl.ds(pl.multiple_of(start, 16), size)

    def spread(n):
        if n < 3:
            return 0, n + 1, 0, 32
        if n < 7:
            return 1, n - 3, 0, 16
        return 2, n - 7, 16, 16

    def expert_rows(s, yy, first, size):
        owner = low if s == 0 else 1 - low
        return rows_at((owner * 4 + yy) * CAP + first, size)

    def buffer_rows(s, yy, first, size):
        return rows_at((0 if s == 0 else 128) + yy * 32 + first, size)

    def scatter(n):
        s, k, first, size = spread(n)
        send(
            packed.at[expert_rows(s, yn[k], first, size)],
            xs.at[z, buffer_rows(s, y, first, size)],
            s_dp.at[n], r_dp.at[n], device(xn[s], yn[k], z, c),
        )

    def x_piece(zz, p):
        return xs.at[zz, buffer_rows(p // 4, yn[p % 4], 0, 32)]

    def dispatch(p):
        k = p % 4
        for n in ((k - 1,) if p < 4 else (3 + k, 7 + k)):
            if n >= 0:
                s, _, first, size = spread(n)
                arrived(xs.at[z, buffer_rows(s, yn[k], first, size)], s_dp.at[n], r_dp.at[n])
        view = x_piece(z, p)
        send(view, view, s_xz.at[p, 0], r_xz.at[p, 0], zdev[1])
        send(view, view, s_xz.at[p, 1], r_xz.at[p, 1], zdev[3])

    def x_forward(p):
        way = p // 4
        view = x_piece(zn[3 if way else 1], p)
        arrived(view, s_xz.at[p, way], r_xz.at[p, way])
        send(view, view, s_xf.at[p], r_xf.at[p], zdev[1 if way else 3])

    def x_rest():
        for p in range(8):
            way = 1 - p // 4
            arrived(x_piece(zn[3 if way else 1], p), s_xz.at[p, way], r_xz.at[p, way])
        for p in range(8):
            arrived(x_piece(zn[2], p), s_xf.at[p], r_xf.at[p])

    def outer_step(o, m, a, b):
        pseudo = o - (a.astype(F32) + b.astype(F32)) / 2
        new_m = momentum_rate * m + pseudo
        return o - outer_rate * (pseudo + momentum_rate * new_m), new_m

    def share(name, n, kind):
        step = STEPS.index((name, n))
        view = fresh_view(step, kind)
        if name == "g":
            send(view, view, s_sg.at[n, kind], r_sg.at[n, kind], sibling)
        else:
            send(view, view, s_sd.at[n, kind, 0], r_sd.at[n, kind, 0], sibling)

    def d_send(n, kind):
        view = wd_view(n, kind, z, c)
        send(view, view, s_dz.at[n, kind, 0], r_dz.at[n, kind, 0], zdev[1])
        send(view, view, s_dz.at[n, kind, 1], r_dz.at[n, kind, 1], zdev[3])

    def update(name, n):
        step = STEPS.index((name, n))
        for copy in loads[step]:
            copy.wait()
        arrived(half_view(rg, rd, step), s_rs.at[step], r_rs.at[step])
        for i in range(2 if name == "g" else 3):

            @pl.loop(0, 4)
            def _(t):
                rows = pl.ds(pl.multiple_of(t * 16, 16), 16)
                if name == "g":
                    at = (i, n, rows, slice(None))
                    a, b = og[n, i, rows, :], rg[n, i, rows, :]
                else:
                    at = (2, i, rows, pl.ds(STARTS[n], WIDTHS[n]))
                    a, b = od[i, rows, pl.ds(STARTS[n], WIDTHS[n])], rd[i, rows, pl.ds(STARTS[n], WIDTHS[n])]
                new_o, new_m = outer_step(ob[at], mb[at], a, b)
                ob[at] = new_o
                mb[at] = new_m
                if name == "g":
                    wg[n, i, c, rows, pl.ds(mine, HALF)] = new_o.astype(BF16)
                else:
                    wd[z, i, c, rows, pl.ds(mine + STARTS[n], WIDTHS[n])] = new_o.astype(BF16)

        view = fresh_view(step, 0)
        send(view, view, s_ag.at[step], r_ag.at[step], partner)
        share(name, n, 0)

    def gathered(name, n):
        step = STEPS.index((name, n))
        arrived(fresh_view(step, 1), s_ag.at[step], r_ag.at[step])
        share(name, n, 1)

    def d_near(n, kind, way):
        view = wd_view(n, kind, zn[3 if way else 1], c)
        arrived(view, s_dz.at[n, kind, way], r_dz.at[n, kind, way])
        if way == kind:
            send(view, view, s_df.at[n, kind], r_df.at[n, kind], zdev[1 if way else 3])
        send(view, view, s_sd.at[n, kind, 1 + way], r_sd.at[n, kind, 1 + way], sibling)

    def d_far(n, kind):
        view = wd_view(n, kind, zn[2], c)
        arrived(view, s_df.at[n, kind], r_df.at[n, kind])
        send(view, view, s_sd.at[n, kind, 3], r_sd.at[n, kind, 3], sibling)

    def hid_cols(zz, n):
        return pl.ds(pl.multiple_of((zz * 3 + n) * 128, 128), 128)

    def hidden(n):
        for kind in (0, 1):
            arrived(wg_view(n, kind, 1 - c), s_sg.at[n, kind], r_sg.at[n, kind])

        @pl.loop(0, 4)
        def _(r):
            zz = turn(z, (r + 1) * (1 + 2 * lax.rem(z, 2)))
            both = lax.dot_general(
                xs[zz], wg[n].reshape(256, WIDTH), (((1,), (1,)), ((), ())),
                preferred_element_type=F32,
            )
            gate = both[:, :128]
            value = (gate / (1.0 + jnp.exp(-gate)) * both[:, 128:]).astype(BF16)
            hs[n, r] = value

            @pl.when(r < 3)
            def _():
                pltpu.make_async_remote_copy(
                    src_ref=hs.at[n, r], dst_ref=hid.at[:, hid_cols(z, n)],
                    send_sem=s_h.at[n, r], recv_sem=r_h.at[n, r],
                    device_id=device(x, y, zz, c), device_id_type=MESH,
                ).start()

        hid[:, hid_cols(z, n)] = hs[n, 3]
        for r in range(3):
            sends.append(
                pltpu.make_async_remote_copy(
                    src_ref=hs.at[n, r], dst_ref=hid.at[:, hid_cols(z, n)],
                    send_sem=s_h.at[n, r], recv_sem=r_h.at[n, r],
                    device_id=zdev[r + 1], device_id_type=MESH,
                )
            )

    def hidden_rest():
        for n in range(3):
            for r in range(3):
                arrived(hid.at[:, hid_cols(zn[r + 1], n)], s_h.at[n, r], r_h.at[n, r])

    def project(n):
        for kind in (0, 1):
            for k, near_z in enumerate((0, 1, 3, 2)):
                arrived(
                    wd_view(n, kind, zn[near_z], 1 - c), s_sd.at[n, kind, k], r_sd.at[n, kind, k]
                )
        for h in (0, 1):

            @pl.loop(0, WIDTHS[n] // 256)
            def _(t):
                cols = pl.ds(pl.multiple_of(STARTS[n] + t * 256, 256), 256)
                wide_cols = pl.ds(pl.multiple_of(h * HALF + STARTS[n] + t * 256, 256), 256)
                ys[h, :, cols] = jnp.dot(
                    hid[...], wd[:, :, :, :, wide_cols].reshape(1536, 256),
                    preferred_element_type=F32,
                ).astype(BF16)

        cols = pl.ds(STARTS[n], WIDTHS[n])
        for m in (1, 8, 4, 0, 5, 9, 2, 6, 10, 3, 7):
            s, k, first, size = spread(m)
            send(
                ys.at[:, buffer_rows(s, yn[k], first, size), cols],
                ret.at[:, rows_at((low * 4 + y) * CAP + first, size), cols],
                s_rt.at[n, m], r_rt.at[n, m], device(xn[s], yn[k], z, c),
            )
        ret[:, expert_rows(0, y, 0, 32), cols] = ys[:, buffer_rows(0, y, 0, 32), cols]

    def finish(n):
        cols = pl.ds(STARTS[n], WIDTHS[n])
        for m in range(11):
            s, k, first, size = spread(m)
            arrived(
                ret.at[:, expert_rows(s, yn[k], first, size), cols],
                s_rt.at[n, m], r_rt.at[n, m],
            )
        for h in (0, 1):
            picked = jnp.dot(place[...], ret[h, :, cols], preferred_element_type=F32)
            wide_cols = pl.ds(h * HALF + STARTS[n], WIDTHS[n])
            eov[:, wide_cols] = (weight[...] * picked).astype(BF16)

    pack()
    pl.semaphore_wait(barrier, len(near))
    actions = (
        start_rs, scatter, dispatch, x_forward, x_rest, update, gathered, d_send, d_near,
        d_far, hidden, hidden_rest, project, finish,
    )
    actions = {action.__name__: action for action in actions}
    for name, *parts in SCHEDULE:
        actions[name](*parts)

    for copy in sends:
        copy.wait_send()


def store(eov, ob, mb, eo, no, nm, sem):
    copies = [pltpu.make_async_copy(eov, eo, sem.at[0])]
    for m in range(3):
        copies.append(pltpu.make_async_copy(ob.at[m], no.at[m], sem.at[1 + m]))
        copies.append(pltpu.make_async_copy(mb.at[m], nm.at[m], sem.at[4 + m]))
    for copy in copies:
        copy.start()
    for copy in copies:
        copy.wait()


def per_device(tokens, expert_ids, route_weight, inner_weights, outer_weights, momentum):
    dma = pltpu.SemaphoreType.DMA
    vmem = pltpu.VMEM
    any_space = pl.BlockSpec(memory_space=pl.ANY)
    in_vmem = pl.BlockSpec(memory_space=pltpu.VMEM)
    weights = (3, 3, 64, HALF)
    scratch = [
        vmem((128, WIDTH), BF16),
        vmem((BLOCK, WIDTH), BF16),
        vmem((4, BLOCK, WIDTH), BF16),
        vmem((3, 2, 2, 64, WIDTH), BF16),
        vmem((4, 3, 2, 64, WIDTH), BF16),
        vmem((3, 2, 64, HALF), BF16),
        vmem((3, 64, HALF), BF16),
        vmem((3, 2, 64, HALF), BF16),
        vmem((3, 64, HALF), BF16),
        vmem((3, 4, BLOCK, 128), BF16),
        vmem((BLOCK, 1536), BF16),
        vmem((2, BLOCK, HALF), BF16),
        vmem((2, BLOCK, HALF), BF16),
        vmem((128, BLOCK), BF16),
        vmem((128, 1), F32),
    ]
    scratch += [dma((len(STEPS),))] * 4
    scratch += [dma((len(STEPS), 3))]
    scratch += [dma((3, 2))] * 2
    scratch += [dma((PARTS, 2, 2))] * 2
    scratch += [dma((PARTS, 2))] * 2
    scratch += [dma((PARTS, 2, 4))] * 2
    scratch += [dma((11,))] * 2
    scratch += [dma((8, 2))] * 2
    scratch += [dma((8,))] * 2
    scratch += [dma((3, 3))] * 2
    scratch += [dma((PARTS, 11))] * 2
    scratch += [dma]
    out, new_outer, new_momentum = pl.pallas_call(
        kernel,
        out_shape=(
            vmem((128, WIDTH), BF16),
            vmem(weights, F32),
            vmem(weights, F32),
        ),
        in_specs=[any_space, in_vmem, in_vmem, any_space, any_space, any_space],
        out_specs=(in_vmem,) * 3,
        scratch_shapes=scratch,
        compiler_params=pltpu.CompilerParams(
            collective_id=0, has_side_effects=True, vmem_limit_bytes=49 << 20
        ),
    )(
        tokens.reshape(128, WIDTH),
        expert_ids.reshape(1, 128),
        route_weight.reshape(1, 128),
        inner_weights.reshape(3, 3, 64, WIDTH),
        outer_weights.reshape(weights),
        momentum.reshape(weights),
    )
    out, new_outer, new_momentum = pl.pallas_call(
        store,
        out_shape=(
            jax.ShapeDtypeStruct((128, WIDTH), BF16),
            jax.ShapeDtypeStruct(weights, F32),
            jax.ShapeDtypeStruct(weights, F32),
        ),
        in_specs=[in_vmem] * 3,
        out_specs=(any_space,) * 3,
        scratch_shapes=[dma((7,))],
        compiler_params=pltpu.CompilerParams(vmem_limit_bytes=40 << 20),
    )(out, new_outer, new_momentum)
    full = (3, 192, HALF)
    return out[None], new_outer.reshape(full), new_momentum.reshape(full)


def solution(mesh):
    in_specs = (
        P("group", "expert", None),
        P("group", "expert", None),
        P("group", "expert", None),
        P("group", None, "expert", None),
        P(None, "expert", "group"),
        P(None, "expert", "group"),
    )
    out_specs = (P("group", "expert", None), P(None, "expert", "group"), P(None, "expert", "group"))
    return jax.shard_map(
        per_device, mesh=mesh, in_specs=in_specs, out_specs=out_specs, check_vma=False
    )
```

```python
import functools

import jax
import jax.numpy as jnp
from jax import lax
from jax.experimental import pallas as pl
from jax.experimental.pallas import tpu as pltpu
from jax.sharding import PartitionSpec as P

MESH = pl.DeviceIdType.MESH
F32 = jnp.float32
BF16 = jnp.bfloat16

outer_rate = 0.7
momentum_rate = 0.9

WIDTH = 4096
HALF = 2048
CAP = 32
WIDTHS = (512, 512, 512, 512)
PARTS = len(WIDTHS)
STARTS = [sum(WIDTHS[:n]) for n in range(PARTS)]
BLOCK = 256
GATES = 3
STEPS = [("g", n) for n in range(GATES)] + [("d", n) for n in range(PARTS)]

SCHEDULE = (
    ("start_rs", "d", 1),
    ("dispatch", 0),
    ("scatter", 0),
    ("start_rs", "d", 0),
    ("start_rs", "d", 3),
    ("scatter", 7),
    ("scatter", 2),
    ("update", "d", 1),
    ("d_send", 1, 0),
    ("update", "d", 0),
    ("d_send", 0, 0),
    ("dispatch", 1),
    ("dispatch", 3),
    ("scatter", 3),
    ("gathered", "d", 1),
    ("gathered", "d", 0),
    ("scatter", 4),
    ("scatter", 8),
    ("dispatch", 4),
    ("scatter", 10),
    ("d_near", 1, 0, 1),
    ("d_send", 1, 1),
    ("update", "d", 3),
    ("d_send", 0, 1),
    ("scatter", 6),
    ("scatter", 9),
    ("d_send", 3, 0),
    ("start_rs", "g", 0),
    ("dispatch", 5),
    ("scatter", 1),
    ("d_near", 0, 0, 0),
    ("x_forward", 4),
    ("x_forward", 3),
    ("dispatch", 2),
    ("start_rs", "g", 1),
    ("d_near", 0, 1, 1),
    ("dispatch", 7),
    ("scatter", 5),
    ("x_forward", 0),
    ("update", "g", 0),
    ("gathered", "d", 3),
    ("x_forward", 5),
    ("dispatch", 6),
    ("d_near", 0, 0, 1),
    ("start_rs", "g", 2),
    ("x_forward", 1),
    ("update", "g", 1),
    ("gathered", "g", 0),
    ("d_send", 3, 1),
    ("x_forward", 2),
    ("d_near", 1, 0, 0),
    ("d_near", 3, 0, 1),
    ("d_near", 3, 0, 0),
    ("x_forward", 7),
    ("x_forward", 6),
    ("update", "g", 2),
    ("d_far", 0, 1),
    ("d_near", 3, 1, 1),
    ("gathered", "g", 1),
    ("d_near", 1, 1, 1),
    ("x_rest",),
    ("d_far", 0, 0),
    ("hidden", 0),
    ("hidden", 1),
    ("gathered", "g", 2),
    ("start_rs", "d", 2),
    ("d_far", 1, 0),
    ("d_near", 3, 1, 0),
    ("d_near", 0, 1, 0),
    ("d_far", 1, 1),
    ("hidden", 2),
    ("update", "d", 2),
    ("d_send", 2, 0),
    ("hidden_rest",),
    ("project", 0),
    ("gathered", "d", 2),
    ("d_near", 1, 1, 0),
    ("d_far", 3, 0),
    ("d_send", 2, 1),
    ("d_near", 2, 0, 0),
    ("d_far", 3, 1),
    ("project", 1),
    ("d_near", 2, 1, 1),
    ("project", 3),
    ("d_near", 2, 0, 1),
    ("d_near", 2, 1, 0),
    ("d_far", 2, 0),
    ("d_far", 2, 1),
    ("project", 2),
    ("finish", 3),
    ("finish", 1),
    ("finish", 0),
    ("finish", 2),
)


def kernel(
    tok, ids, rw, inner, outer, mom, eov, ob, mb,
    tokv, packed, xs, wg, wd, rg, rd, og, od, hs, hid, ys, ret, place, weight,
    s_rs, r_rs, s_ag, r_ag, l_in, s_sg, r_sg, s_dz, r_dz, s_df, r_df, s_sd, r_sd,
    s_dp, r_dp, s_xz, r_xz, s_xf, r_xf, s_h, r_h, s_rt, r_rt, l_tok,
):
    g = lax.axis_index("group")
    e = lax.axis_index("expert")
    low = lax.div(e, 32)
    y = lax.rem(lax.div(e, 8), 4)
    z = lax.rem(lax.div(e, 2), 4)
    c = lax.rem(e, 2)
    x = g * 2 + low

    def device(xx, yy, zz, cc):
        return (lax.div(xx, 2), ((lax.rem(xx, 2) * 4 + yy) * 4 + zz) * 2 + cc)

    def turn(a, n):
        return lax.rem(a + n, 4)

    def around(a):
        way = 1 + 2 * lax.rem(a, 2)
        return a, turn(a, way), turn(a, 2), turn(a, 4 - way)

    ring, yn, zn = around(x), around(y), around(z)
    xn = (ring[0], ring[1], ring[3])
    partner = device(ring[2], y, z, c)
    sibling = device(x, y, z, 1 - c)
    zdev = [device(x, y, zz, c) for zz in zn]

    barrier = pltpu.get_barrier_semaphore()
    near = [partner, sibling] + zdev[1:]
    near += [device(x, yn[k], z, c) for k in (1, 2, 3)]
    near += [device(xn[s], yn[k], z, c) for s in (1, 2) for k in range(4)]
    for other in near:
        pl.semaphore_signal(barrier, inc=1, device_id=other, device_id_type=MESH)

    sends = []

    def send(src, dst, ss, rs, dev):
        copy = pltpu.make_async_remote_copy(
            src_ref=src, dst_ref=dst, send_sem=ss, recv_sem=rs, device_id=dev, device_id_type=MESH
        )
        copy.start()
        sends.append(copy)

    def arrived(dst, ss, rs):
        pltpu.make_async_remote_copy(
            src_ref=dst, dst_ref=dst, send_sem=ss, recv_sem=rs, device_id=sibling, device_id_type=MESH
        ).wait_recv()

    def local(src, dst, sem):
        copy = pltpu.make_async_copy(src, dst, sem)
        copy.start()
        return copy

    mine = pl.multiple_of(g * HALF, HALF)
    theirs = pl.multiple_of((1 - g) * HALF, HALF)
    half_of = (mine, theirs)

    def in_view(ref, step, offset):
        kind, n = STEPS[step]
        if kind == "g":
            return ref.at[0:2, n, :, pl.ds(offset, HALF)]
        return ref.at[2, :, :, pl.ds(offset + STARTS[n], WIDTHS[n])]

    def half_view(ref_g, ref_d, step):
        kind, n = STEPS[step]
        if kind == "g":
            return ref_g.at[n]
        return ref_d.at[:, :, pl.ds(STARTS[n], WIDTHS[n])]

    def wg_view(n, kind, core):
        return wg.at[n, :, core, :, pl.ds(half_of[kind], HALF)]

    def wd_view(n, kind, zz, core):
        return wd.at[zz, :, core, :, pl.ds(half_of[kind] + STARTS[n], WIDTHS[n])]

    def fresh_view(step, kind):
        name, n = STEPS[step]
        return wg_view(n, kind, c) if name == "g" else wd_view(n, kind, z, c)

    tok_copy = local(tok, tokv, l_tok)
    loads = {}
    for name, *part in SCHEDULE:
        if name == "update":
            step = STEPS.index(tuple(part))
            loads[step] = (
                local(in_view(inner, step, mine), half_view(og, od, step), l_in.at[step, 0]),
                local(in_view(outer, step, 0), in_view(ob, step, 0), l_in.at[step, 1]),
                local(in_view(mom, step, 0), in_view(mb, step, 0), l_in.at[step, 2]),
            )

    def pack():
        lane = lax.broadcasted_iota(jnp.int32, (128, 128), 1)
        row = lax.broadcasted_iota(jnp.int32, (128, 128), 0)
        named = ids[...]
        one_hot = (row == named).astype(F32)
        earlier = (row < lane).astype(BF16)
        rank = jnp.dot(one_hot.astype(BF16), earlier, preferred_element_type=F32)
        rank = jnp.sum(rank * one_hot, axis=0, keepdims=True)
        slot = named.astype(F32) * CAP + rank
        tall = lax.broadcasted_iota(jnp.int32, (BLOCK, 128), 0).astype(F32)
        placing = (tall == slot).astype(F32)
        place[...] = jnp.transpose(placing).astype(BF16)
        weight[...] = jnp.sum(jnp.where(lane == row, rw[...], 0.0), axis=1, keepdims=True)
        tok_copy.wait()

        @pl.loop(0, WIDTH // 512)
        def _(n):
            cols = pl.ds(pl.multiple_of(n * 512, 512), 512)
            packed[:, cols] = jnp.dot(
                placing.astype(BF16), tokv[:, cols], preferred_element_type=F32
            ).astype(BF16)

        xs[z, rows_at(y * 32, 32), :] = packed[expert_rows(0, y, 0, 32), :]

    def start_rs(name, n):
        step = STEPS.index((name, n))
        send(
            in_view(inner, step, theirs), half_view(rg, rd, step),
            s_rs.at[step], r_rs.at[step], partner,
        )

    def rows_at(start, size):
        return pl.ds(pl.multiple_of(start, 16), size)

    def spread(n):
        if n < 3:
            return 0, n + 1, 0, 32
        if n < 7:
            return 1, n - 3, 0, 16
        return 2, n - 7, 16, 16

    def expert_rows(s, yy, first, size):
        owner = low if s == 0 else 1 - low
        return rows_at((owner * 4 + yy) * CAP + first, size)

    def buffer_rows(s, yy, first, size):
        return rows_at((0 if s == 0 else 128) + yy * 32 + first, size)

    def scatter(n):
        s, k, first, size = spread(n)
        send(
            packed.at[expert_rows(s, yn[k], first, size)],
            xs.at[z, buffer_rows(s, y, first, size)],
            s_dp.at[n], r_dp.at[n], device(xn[s], yn[k], z, c),
        )

    def x_piece(zz, p):
        return xs.at[zz, buffer_rows(p // 4, yn[p % 4], 0, 32)]

    def dispatch(p):
        k = p % 4
        for n in ((k - 1,) if p < 4 else (3 + k, 7 + k)):
            if n >= 0:
                s, _, first, size = spread(n)
                arrived(xs.at[z, buffer_rows(s, yn[k], first, size)], s_dp.at[n], r_dp.at[n])
        view = x_piece(z, p)
        send(view, view, s_xz.at[p, 0], r_xz.at[p, 0], zdev[1])
        send(view, view, s_xz.at[p, 1], r_xz.at[p, 1], zdev[3])

    def x_forward(p):
        way = p // 4
        view = x_piece(zn[3 if way else 1], p)
        arrived(view, s_xz.at[p, way], r_xz.at[p, way])
        send(view, view, s_xf.at[p], r_xf.at[p], zdev[1 if way else 3])

    def x_rest():
        for p in range(8):
            way = 1 - p // 4
            arrived(x_piece(zn[3 if way else 1], p), s_xz.at[p, way], r_xz.at[p, way])
        for p in range(8):
            arrived(x_piece(zn[2], p), s_xf.at[p], r_xf.at[p])

    def outer_step(o, m, a, b):
        pseudo = o - (a.astype(F32) + b.astype(F32)) / 2
        new_m = momentum_rate * m + pseudo
        return o - outer_rate * (pseudo + momentum_rate * new_m), new_m

    def share(name, n, kind):
        step = STEPS.index((name, n))
        view = fresh_view(step, kind)
        if name == "g":
            send(view, view, s_sg.at[n, kind], r_sg.at[n, kind], sibling)
        else:
            send(view, view, s_sd.at[n, kind, 0], r_sd.at[n, kind, 0], sibling)

    def d_send(n, kind):
        view = wd_view(n, kind, z, c)
        send(view, view, s_dz.at[n, kind, 0], r_dz.at[n, kind, 0], zdev[1])
        send(view, view, s_dz.at[n, kind, 1], r_dz.at[n, kind, 1], zdev[3])

    def update(name, n):
        step = STEPS.index((name, n))
        for copy in loads[step]:
            copy.wait()
        arrived(half_view(rg, rd, step), s_rs.at[step], r_rs.at[step])
        for i in range(2 if name == "g" else 3):

            @pl.loop(0, 4)
            def _(t):
                rows = pl.ds(pl.multiple_of(t * 16, 16), 16)
                if name == "g":
                    at = (i, n, rows, slice(None))
                    a, b = og[n, i, rows, :], rg[n, i, rows, :]
                else:
                    at = (2, i, rows, pl.ds(STARTS[n], WIDTHS[n]))
                    a, b = od[i, rows, pl.ds(STARTS[n], WIDTHS[n])], rd[i, rows, pl.ds(STARTS[n], WIDTHS[n])]
                new_o, new_m = outer_step(ob[at], mb[at], a, b)
                ob[at] = new_o
                mb[at] = new_m
                if name == "g":
                    wg[n, i, c, rows, pl.ds(mine, HALF)] = new_o.astype(BF16)
                else:
                    wd[z, i, c, rows, pl.ds(mine + STARTS[n], WIDTHS[n])] = new_o.astype(BF16)

        view = fresh_view(step, 0)
        send(view, view, s_ag.at[step], r_ag.at[step], partner)
        share(name, n, 0)

    def gathered(name, n):
        step = STEPS.index((name, n))
        arrived(fresh_view(step, 1), s_ag.at[step], r_ag.at[step])
        share(name, n, 1)

    def d_near(n, kind, way):
        view = wd_view(n, kind, zn[3 if way else 1], c)
        arrived(view, s_dz.at[n, kind, way], r_dz.at[n, kind, way])
        if way == kind:
            send(view, view, s_df.at[n, kind], r_df.at[n, kind], zdev[1 if way else 3])
        send(view, view, s_sd.at[n, kind, 1 + way], r_sd.at[n, kind, 1 + way], sibling)

    def d_far(n, kind):
        view = wd_view(n, kind, zn[2], c)
        arrived(view, s_df.at[n, kind], r_df.at[n, kind])
        send(view, view, s_sd.at[n, kind, 3], r_sd.at[n, kind, 3], sibling)

    def hid_cols(zz, n):
        return pl.ds(pl.multiple_of((zz * 3 + n) * 128, 128), 128)

    def hidden(n):
        for kind in (0, 1):
            arrived(wg_view(n, kind, 1 - c), s_sg.at[n, kind], r_sg.at[n, kind])

        @pl.loop(0, 4)
        def _(r):
            zz = turn(z, (r + 1) * (1 + 2 * lax.rem(z, 2)))
            both = lax.dot_general(
                xs[zz], wg[n].reshape(256, WIDTH), (((1,), (1,)), ((), ())),
                preferred_element_type=F32,
            )
            gate = both[:, :128]
            value = (gate / (1.0 + jnp.exp(-gate)) * both[:, 128:]).astype(BF16)
            hs[n, r] = value

            @pl.when(r < 3)
            def _():
                pltpu.make_async_remote_copy(
                    src_ref=hs.at[n, r], dst_ref=hid.at[:, hid_cols(z, n)],
                    send_sem=s_h.at[n, r], recv_sem=r_h.at[n, r],
                    device_id=device(x, y, zz, c), device_id_type=MESH,
                ).start()

        hid[:, hid_cols(z, n)] = hs[n, 3]
        for r in range(3):
            sends.append(
                pltpu.make_async_remote_copy(
                    src_ref=hs.at[n, r], dst_ref=hid.at[:, hid_cols(z, n)],
                    send_sem=s_h.at[n, r], recv_sem=r_h.at[n, r],
                    device_id=zdev[r + 1], device_id_type=MESH,
                )
            )

    def hidden_rest():
        for n in range(3):
            for r in range(3):
                arrived(hid.at[:, hid_cols(zn[r + 1], n)], s_h.at[n, r], r_h.at[n, r])

    def project(n):
        for kind in (0, 1):
            for k, near_z in enumerate((0, 1, 3, 2)):
                arrived(
                    wd_view(n, kind, zn[near_z], 1 - c), s_sd.at[n, kind, k], r_sd.at[n, kind, k]
                )
        for h in (0, 1):

            @pl.loop(0, WIDTHS[n] // 256)
            def _(t):
                cols = pl.ds(pl.multiple_of(STARTS[n] + t * 256, 256), 256)
                wide_cols = pl.ds(pl.multiple_of(h * HALF + STARTS[n] + t * 256, 256), 256)
                ys[h, :, cols] = jnp.dot(
                    hid[...], wd[:, :, :, :, wide_cols].reshape(1536, 256),
                    preferred_element_type=F32,
                ).astype(BF16)

        cols = pl.ds(STARTS[n], WIDTHS[n])
        for m in (1, 8, 4, 0, 5, 9, 2, 6, 10, 3, 7):
            s, k, first, size = spread(m)
            send(
                ys.at[:, buffer_rows(s, yn[k], first, size), cols],
                ret.at[:, rows_at((low * 4 + y) * CAP + first, size), cols],
                s_rt.at[n, m], r_rt.at[n, m], device(xn[s], yn[k], z, c),
            )
        ret[:, expert_rows(0, y, 0, 32), cols] = ys[:, buffer_rows(0, y, 0, 32), cols]

    def finish(n):
        cols = pl.ds(STARTS[n], WIDTHS[n])
        for m in range(11):
            s, k, first, size = spread(m)
            arrived(
                ret.at[:, expert_rows(s, yn[k], first, size), cols],
                s_rt.at[n, m], r_rt.at[n, m],
            )
        for h in (0, 1):
            picked = jnp.dot(place[...], ret[h, :, cols], preferred_element_type=F32)
            wide_cols = pl.ds(h * HALF + STARTS[n], WIDTHS[n])
            eov[:, wide_cols] = (weight[...] * picked).astype(BF16)

    pack()
    pl.semaphore_wait(barrier, len(near))
    actions = (
        start_rs, scatter, dispatch, x_forward, x_rest, update, gathered, d_send, d_near,
        d_far, hidden, hidden_rest, project, finish,
    )
    actions = {action.__name__: action for action in actions}
    for name, *parts in SCHEDULE[:-1]:
        actions[name](*parts)
    for copy in sends:
        copy.wait_send()
    name, *parts = SCHEDULE[-1]
    actions[name](*parts)


def store(eov, ob, mb, eo, no, nm, sem):
    copies = [pltpu.make_async_copy(eov, eo, sem.at[0])]
    for m in range(3):
        copies.append(pltpu.make_async_copy(ob.at[m], no.at[m], sem.at[1 + m]))
        copies.append(pltpu.make_async_copy(mb.at[m], nm.at[m], sem.at[4 + m]))
    for copy in copies:
        copy.start()
    for copy in copies:
        copy.wait()


def per_device(tokens, expert_ids, route_weight, inner_weights, outer_weights, momentum):
    dma = pltpu.SemaphoreType.DMA
    vmem = pltpu.VMEM
    any_space = pl.BlockSpec(memory_space=pl.ANY)
    in_vmem = pl.BlockSpec(memory_space=pltpu.VMEM)
    weights = (3, 3, 64, HALF)
    scratch = [
        vmem((128, WIDTH), BF16),
        vmem((BLOCK, WIDTH), BF16),
        vmem((4, BLOCK, WIDTH), BF16),
        vmem((3, 2, 2, 64, WIDTH), BF16),
        vmem((4, 3, 2, 64, WIDTH), BF16),
        vmem((3, 2, 64, HALF), BF16),
        vmem((3, 64, HALF), BF16),
        vmem((3, 2, 64, HALF), BF16),
        vmem((3, 64, HALF), BF16),
        vmem((3, 4, BLOCK, 128), BF16),
        vmem((BLOCK, 1536), BF16),
        vmem((2, BLOCK, HALF), BF16),
        vmem((2, BLOCK, HALF), BF16),
        vmem((128, BLOCK), BF16),
        vmem((128, 1), F32),
    ]
    scratch += [dma((len(STEPS),))] * 4
    scratch += [dma((len(STEPS), 3))]
    scratch += [dma((3, 2))] * 2
    scratch += [dma((PARTS, 2, 2))] * 2
    scratch += [dma((PARTS, 2))] * 2
    scratch += [dma((PARTS, 2, 4))] * 2
    scratch += [dma((11,))] * 2
    scratch += [dma((8, 2))] * 2
    scratch += [dma((8,))] * 2
    scratch += [dma((3, 3))] * 2
    scratch += [dma((PARTS, 11))] * 2
    scratch += [dma]
    out, new_outer, new_momentum = pl.pallas_call(
        kernel,
        out_shape=(
            vmem((128, WIDTH), BF16),
            vmem(weights, F32),
            vmem(weights, F32),
        ),
        in_specs=[any_space, in_vmem, in_vmem, any_space, any_space, any_space],
        out_specs=(in_vmem,) * 3,
        scratch_shapes=scratch,
        compiler_params=pltpu.CompilerParams(
            collective_id=0, has_side_effects=True, vmem_limit_bytes=49 << 20
        ),
    )(
        tokens.reshape(128, WIDTH),
        expert_ids.reshape(1, 128),
        route_weight.reshape(1, 128),
        inner_weights.reshape(3, 3, 64, WIDTH),
        outer_weights.reshape(weights),
        momentum.reshape(weights),
    )
    out, new_outer, new_momentum = pl.pallas_call(
        store,
        out_shape=(
            jax.ShapeDtypeStruct((128, WIDTH), BF16),
            jax.ShapeDtypeStruct(weights, F32),
            jax.ShapeDtypeStruct(weights, F32),
        ),
        in_specs=[in_vmem] * 3,
        out_specs=(any_space,) * 3,
        scratch_shapes=[dma((7,))],
        compiler_params=pltpu.CompilerParams(vmem_limit_bytes=40 << 20),
    )(out, new_outer, new_momentum)
    full = (3, 192, HALF)
    return out[None], new_outer.reshape(full), new_momentum.reshape(full)


def solution(mesh):
    in_specs = (
        P("group", "expert", None),
        P("group", "expert", None),
        P("group", "expert", None),
        P("group", None, "expert", None),
        P(None, "expert", "group"),
        P(None, "expert", "group"),
    )
    out_specs = (P("group", "expert", None), P(None, "expert", "group"), P(None, "expert", "group"))
    return jax.shard_map(
        per_device, mesh=mesh, in_specs=in_specs, out_specs=out_specs, check_vma=False
    )
```
